128 devices in a mesh: vec: 8 (over y, x_lo), walk: 16 (over x_hi, z, core).
Axes of the slice: x: 4 (x_hi: 2, x_lo: 2; x = x_hi * 2 + x_lo), y: 4, z: 4, core: 2. Of those that a mesh axis runs over, the one named last changes fastest.
Arguments:
- walkers: bfloat16 [256, 1024, 128], P('walk', 'vec'), may hold values from -6 to 6
- inverse: bfloat16 [256, 2, 2, 32, 32], P('walk'), may hold values from -0.75 to 0.75
- vectors: bfloat16 [10240, 1024, 128], P('walk', 'vec'), may hold values from -0.015625 to 0.015625
- sources: int32 [256], replicated, may hold values from 0 to 255
Outputs:
- moved: bfloat16 [256, 1024, 128], P('walk', 'vec')
- force_bias: float32 [2, 256, 10240], P(None, 'vec', 'walk')
The draws below stay inside these ranges and needn't reach their ends.
Inputs may be any that keep to these rules, and one draw needn't show every extreme that they name: New walker j is a copy of old walker sources[j]; an old walker may be copied many times or not at all.
All inputs are finite; a program needn't handle non-finite values.
Results may differ from the reference program's by a relative error of at most 0.0029.
Values may be sent and summed in bfloat16 or wider, within the bound.
No kernel may reach another device: no remote copies, remote signals or barrier semaphores. Data moves between devices by JAX's collectives and lax.ppermute only.
A program may use at most 192 MiB of HBM per device.

```python
import math
import jax
import jax.numpy as jnp
import numpy as np
from jax import lax

M = 1024
NOCC = 32
NCHOL = 10240
W = 256


def set_ends(array, key, smallest, top_value):
    index_at = [jax.random.randint(jax.random.fold_in(key, axis), (), 0, length) for axis, length in enumerate(array.shape)]
    widest = array.shape.index(max(array.shape))
    next_to = index_at[:widest] + [(index_at[widest] + 1) % array.shape[widest]] + index_at[widest + 1:]
    return array.at[tuple(index_at)].set(smallest).at[tuple(next_to)].set(top_value)


def shard_levels(stream_key, shape, shards, smallest, largest):
    factor_of, own = 1.0, jax.random.fold_in(stream_key, 6)
    for position, blocks in shards:
        heights = jnp.exp(jax.random.uniform(jax.random.fold_in(own, position), (blocks,), jnp.float32, smallest / len(shards), largest / len(shards)))
        factor_of = factor_of * jnp.repeat(heights, shape[position] // blocks).reshape([-1 if axis == position else 1 for axis in range(len(shape))])
    return factor_of


def rank_table(number_of, slope):
    weights = [(1 << 20) // math.isqrt(standing ** slope) + 1 for standing in range(1, number_of + 1)]
    scale = 1 + sum(weights) // (1 << 30)
    return np.cumsum(np.array([max(1, weight // scale) for weight in weights]))


def skewed_ids(stream_key, dims, amount, slope):
    listing = rank_table(amount, slope)
    pick = jax.random.randint(jax.random.fold_in(stream_key, 1), dims, 0, int(listing[amount - 1]))
    standing = jnp.searchsorted(jnp.asarray(listing, jnp.int32), pick, side="right")
    return jax.random.permutation(jax.random.fold_in(stream_key, 2), amount)[standing].astype(jnp.int32)


def centred(own_key, dims, spread, bound, cuts=(), dtype=jnp.bfloat16):
    values = spread * jax.random.normal(own_key, dims, jnp.float32)
    if cuts:
        values = values * shard_levels(own_key, dims, cuts, -0.22, 0.18)
    return jnp.clip(values, -bound, bound).astype(dtype)


def setup_inputs(seed: int = 0) -> dict:
    splits = jax.random.split(jax.random.key(seed), 5)
    return {
        "walkers": centred(splits[0], (W, M, 4 * NOCC), 1.0, 6.0, ((0, 16), (1, 8))),
        "inverse": centred(splits[1], (W, 2, 2, NOCC, NOCC), 0.125, 0.75, ((0, 16),)),
        "vectors": centred(splits[2], (NCHOL, M, 4 * NOCC), (M * 4 * NOCC) ** -0.5, 0.015625, ((0, 16), (1, 8))),
        "sources": set_ends(skewed_ids(splits[3], (W,), W, 2), jax.random.fold_in(splits[3], 3), 0, W - 1).astype(jnp.int32),
    }


def block_of(part):
    real_part, imag_part = part[:, 0], part[:, 1]
    first = jnp.stack([real_part, imag_part], 3)
    second = jnp.stack([-imag_part, real_part], 3)
    return jnp.stack([first, second], 2)


def green(moved, moved_inverse):
    count, orbitals = moved.shape[0], moved.shape[1]
    operator = block_of(moved_inverse).astype(jnp.float32)
    parts = moved.reshape(count, orbitals, 2, 2, -1).astype(jnp.float32)
    theta = jnp.einsum('wpcsk,wsckdi->wpdsi', parts, operator, precision=lax.Precision.HIGHEST)
    return theta.reshape(count, orbitals, -1).astype(jnp.bfloat16)


def rows_of(theta):
    count, orbitals = theta.shape[0], theta.shape[1]
    split = theta.reshape(count, orbitals, 2, -1)
    first = jnp.stack([split[:, :, 0], -split[:, :, 1]], 2).reshape(count, -1)
    second = jnp.stack([split[:, :, 1], split[:, :, 0]], 2).reshape(count, -1)
    return jnp.stack([first, second], 0)


def reference(walkers, inverse, vectors, sources):
    moved = jnp.take(walkers, sources, axis=0)
    moved_inverse = jnp.take(inverse, sources, axis=0)
    theta = green(moved, moved_inverse)
    stacked = rows_of(theta).reshape(2 * W, -1)
    block = math.gcd(NCHOL, 1024)
    blocks = vectors.reshape(NCHOL // block, block, -1)

    def one_block(piece):
        return lax.dot_general(stacked, piece, (((1,), (1,)), ((), ())), preferred_element_type=jnp.float32)

    result = lax.map(one_block, blocks)
    result = jnp.moveaxis(result, 0, 1).reshape(2, W, NCHOL)
    return moved, result
```

```python
import functools

import jax
import jax.numpy as jnp
from jax import lax
from jax.experimental import pallas as pl
from jax.experimental.pallas import tpu as pltpu
from jax.sharding import PartitionSpec as P

BF = jnp.bfloat16
F32 = jnp.float32


def swap_matrix():
    row = lax.broadcasted_iota(jnp.int32, (256, 256), 0)
    col = lax.broadcasted_iota(jnp.int32, (256, 256), 1)
    hit = (row // 16 == col % 16) & (row % 16 == col // 16)
    return jnp.where(hit, 1.0, 0.0).astype(BF)


def flatten_kernel(v_ref, out_ref):
    swap = swap_matrix()
    for p in range(0, 128, 16):
        pair = [v_ref[g : g + 16, p : p + 16, :].reshape(256, 128) for g in (0, 16)]
        both = jnp.dot(swap, jnp.concatenate(pair, axis=1), preferred_element_type=F32)
        both = both.astype(BF)
        for q in range(16):
            for h in range(2):
                out_ref[h * 16 : h * 16 + 16, (p + q) * 128 : (p + q + 1) * 128] = both[
                    q * 16 : q * 16 + 16, h * 128 : h * 128 + 128
                ]


def flatten_vectors(vectors):
    count = vectors.shape[0]
    return pl.pallas_call(
        flatten_kernel,
        grid=(count // 32,),
        in_specs=[pl.BlockSpec((32, 128, 128), lambda i: (i, 0, 0))],
        out_specs=pl.BlockSpec((32, 16384), lambda i: (i, 0)),
        out_shape=jax.ShapeDtypeStruct((count, 16384), BF),
        compiler_params=pltpu.CompilerParams(vmem_limit_bytes=32 << 20),
        cost_estimate=pl.CostEstimate(
            flops=2 * count * 16384 * 256, bytes_accessed=4 * count * 16384, transcendentals=0
        ),
    )(vectors)


def theta_kernel(split, *refs):
    out_ref, work = refs[-2:]
    refs = refs[:-2]
    swap = swap_matrix()
    lane = lax.broadcasted_iota(jnp.int32, (32, 128), 1)
    sign = jnp.where(lane < 64, 1.0, -1.0)
    keep0 = jnp.where(lane % 64 < 32, 1.0, 0.0)
    keep1 = 1.0 - keep0

    def walker(ref, w, slot):
        small = ref[w, 128:160, :].astype(F32)
        a = small * sign
        b = jnp.concatenate([small[:, 64:], small[:, :64]], axis=1)
        ab = jnp.concatenate([a, b], axis=1)
        ba = jnp.concatenate([-b, a], axis=1)
        k0 = jnp.concatenate([keep0, keep0], axis=1)
        k1 = jnp.concatenate([keep1, keep1], axis=1)
        operator = jnp.concatenate([ab * k0, ab * k1, ba * k0, ba * k1], axis=0).astype(BF)
        work[slot] = jnp.dot(ref[w, 0:128, :], operator, preferred_element_type=F32).astype(BF)

    per = 2 if split else 1
    for half in range(2):
        for n in range(per):
            ref = refs[half * per + n]
            size = 16 // per

            @pl.loop(0, size, unroll=2)
            def _(w):
                walker(ref, w, n * size + w)

        for p in range(0, 128, 16):
            turned = jnp.dot(
                swap, work[:, p : p + 16, :].reshape(256, 256), preferred_element_type=F32
            ).astype(BF)
            for q in range(16):
                for c in range(2):
                    row = c * 32 + half * 16
                    out_ref[row : row + 16, (p + q) * 128 : (p + q + 1) * 128] = turned[
                        q * 16 : q * 16 + 16, c * 128 : c * 128 + 128
                    ]


def theta_of(*pieces):
    return pl.pallas_call(
        functools.partial(theta_kernel, len(pieces) == 4),
        out_shape=jax.ShapeDtypeStruct((64, 16384), BF),
        scratch_shapes=[pltpu.VMEM((16, 128, 256), BF)],
        compiler_params=pltpu.CompilerParams(vmem_limit_bytes=32 << 20),
        cost_estimate=pl.CostEstimate(
            flops=2 * 32 * 16384 * 256 * 2, bytes_accessed=6 << 20, transcendentals=0
        ),
    )(*pieces)


def product_kernel(last, v_ref, *refs):
    thetas = refs[:4]
    pick_ref = refs[4]
    rest = refs[5:]
    acc = rest[-1]
    step = pl.program_id(0)

    @pl.when(step == 0)
    def _():
        acc[...] = jnp.zeros_like(acc)

    theta = jnp.concatenate([t[...] for t in thetas], axis=0)
    acc[...] += lax.dot_general(
        v_ref[...], theta, (((1,), (1,)), ((), ())), preferred_element_type=F32
    )

    @pl.when(step == pl.num_programs(0) - 1)
    def _():
        bias = acc[...].astype(BF)
        picked = lax.dot_general(
            pick_ref[...], bias, (((1,), (1,)), ((), ())), preferred_element_type=F32
        )
        if last:
            rest[1][...] = (picked + rest[0][...]).astype(BF)
        else:
            rest[0][...] = picked


def product(flat, thetas, pick, before=None):
    count = flat.shape[0]
    depth = 1024
    last = before is not None
    extra = [before] if last else []
    whole = lambda shape: pl.BlockSpec(shape, lambda k: (0, 0))
    return pl.pallas_call(
        functools.partial(product_kernel, last),
        grid=(16384 // depth,),
        in_specs=[pl.BlockSpec((count, depth), lambda k: (0, k))]
        + [pl.BlockSpec((64, depth), lambda k: (0, k))] * 4
        + [whole((512, 256))]
        + [whole((512, count))] * len(extra),
        out_specs=whole((512, count)),
        out_shape=jax.ShapeDtypeStruct((512, count), BF if last else F32),
        scratch_shapes=[pltpu.VMEM((count, 256), F32)],
        compiler_params=pltpu.CompilerParams(vmem_limit_bytes=32 << 20),
        cost_estimate=pl.CostEstimate(
            flops=2 * count * 16384 * 256, bytes_accessed=2 * (count + 256) * 16384, transcendentals=0
        ),
    )(flat, *thetas, pick, *extra)


def moved_kernel(sizes, piece_ref, row_ref, *refs):
    sources, out_ref, sem = refs[:-2], refs[-2], refs[-1]
    for j in range(16):
        for n, src in enumerate(sources):

            @pl.when(piece_ref[j] == n)
            def _(j=j, src=src):
                pltpu.make_async_copy(
                    src.at[row_ref[j], pl.ds(0, 128), :], out_ref.at[j], sem.at[j]
                ).start()

    for j in range(16):
        pltpu.make_async_copy(
            sources[0].at[0, pl.ds(0, 128), :], out_ref.at[j], sem.at[j]
        ).wait()


def moved_of(piece, row, pieces):
    sizes = tuple(p.shape[0] for p in pieces)
    return pl.pallas_call(
        functools.partial(moved_kernel, sizes),
        grid_spec=pltpu.PrefetchScalarGridSpec(
            num_scalar_prefetch=2,
            grid=(1,),
            in_specs=[pl.BlockSpec(memory_space=pl.ANY)] * len(pieces),
            out_specs=pl.BlockSpec(memory_space=pl.ANY),
            scratch_shapes=[pltpu.SemaphoreType.DMA((16,))],
        ),
        out_shape=jax.ShapeDtypeStruct((16, 128, 128), BF),
    )(piece, row, *pieces)


def index(x, z, core):
    return (x % 2 * 4 + z % 4) * 2 + core


def moves(step):
    return [
        (index(x, z, c), index(*step(x, z, c))) for x in range(2) for z in range(4) for c in range(2)
    ]


ACROSS = moves(lambda x, z, c: (x + 1, z, c))
UP = moves(lambda x, z, c: (x, z + 1, c))
DOWN = moves(lambda x, z, c: (x, z - 1, c))
OTHER = moves(lambda x, z, c: (x, z, 1 - c))


def send(value, pairs):
    return lax.ppermute(value, "walk", pairs)


def per_device(walkers, inverse, vectors, sources):
    me = lax.axis_index("walk")
    x, z, core = me // 8, me // 2 % 4, me % 2
    small = inverse.transpose(0, 3, 1, 2, 4).reshape(16, 32, 128)
    own = jnp.concatenate([walkers, small], axis=1)
    across = send(own, ACROSS)
    below = send(own, UP)
    above = send(own, DOWN)
    far0 = send(below[:8], UP)
    far1 = send(above[8:], DOWN)
    across_below = send(across, UP)
    across_above = send(across, DOWN)
    across_far0 = send(far0, ACROSS)
    across_far1 = send(far1, ACROSS)

    groups = [
        (0, 0, [own]),
        (1, 0, [across]),
        (0, -1, [below]),
        (0, 1, [above]),
        (0, 2, [far0, far1]),
        (1, -1, [across_below]),
        (1, 1, [across_above]),
        (1, 2, [across_far0, across_far1]),
    ]
    flat = flatten_vectors(vectors)
    old_ids, thetas, pieces, places = [], [], [], []
    sixteen = jnp.arange(16, dtype=jnp.int32)
    for dx, dz, parts in groups:
        both = parts + [send(part, OTHER) for part in parts]
        thetas.append(theta_of(*both))
        ids = []
        for c in (core, 1 - core):
            ids.append(index(x + dx, z + dz, c) * 16 + sixteen)
        old_ids.append(jnp.concatenate(ids))
        per = len(parts)
        base = len(pieces)
        for half in range(2):
            places.append(base + half * per + sixteen * per // 16)
        pieces += both
    vec = lax.axis_index("vec")
    targets = [((vec // 2 + dy) % 4) * 2 + (vec % 2 + dv) % 2 for dy in range(4) for dv in range(2)]
    wanted = jnp.stack([lax.dynamic_slice_in_dim(sources, t * 32, 32) for t in targets])
    picks = []
    for part in range(2):
        ids = jnp.stack(old_ids[4 * part : 4 * part + 4])
        same = wanted[:, None, :, None, None, None] == ids[None, None, None, :, None, :]
        kind = jnp.arange(2)
        same = same & (kind[None, :, None, None, None, None] == kind[None, None, None, None, :, None])
        picks.append(same.astype(BF).reshape(512, 256))
    first = product(flat, thetas[:4], picks[0])
    sums = product(flat, thetas[4:], picks[1], first)

    total = sums[:64].astype(F32)
    for n in range(1, 8):
        dy, dv = n // 2, n % 2
        pairs = [
            (y * 2 + v, ((y + dy) % 4) * 2 + (v + dv) % 2) for y in range(4) for v in range(2)
        ]
        total = total + lax.ppermute(sums[64 * n : 64 * n + 64], "vec", pairs).astype(F32)

    mine = lax.dynamic_slice_in_dim(sources, me * 16, 16)
    table = jnp.concatenate(old_ids)
    slot = jnp.argmax(mine[:, None] == table[None, :], axis=1).astype(jnp.int32)
    piece = jnp.concatenate(places)[slot]
    long = [p.shape[0] for p in pieces]
    row = slot % jnp.asarray(long, jnp.int32)[piece]
    moved = moved_of(piece, row, pieces)
    return (moved, total.reshape(2, 32, -1))


def solution(mesh):
    in_specs = (
        P("walk", "vec", None),
        P("walk", None, None, None, None),
        P("walk", "vec", None),
        P(),
    )
    out_specs = (P("walk", "vec", None), P(None, "vec", "walk"))
    return jax.shard_map(
        per_device, mesh=mesh, in_specs=in_specs, out_specs=out_specs, check_vma=False
    )
```

```python
import functools

import jax
import jax.numpy as jnp
from jax import lax
from jax.experimental import pallas as pl
from jax.experimental.pallas import tpu as pltpu
from jax.sharding import PartitionSpec as P

BF = jnp.bfloat16
F32 = jnp.float32
WHOLE = pl.BlockSpec(memory_space=pltpu.VMEM)


def near(value):
    return pltpu.with_memory_space_constraint(value, pltpu.VMEM)


def swap_matrix():
    row = lax.broadcasted_iota(jnp.int32, (256, 256), 0)
    col = lax.broadcasted_iota(jnp.int32, (256, 256), 1)
    hit = (row // 16 == col % 16) & (row % 16 == col // 16)
    return jnp.where(hit, 1.0, 0.0).astype(BF)


def flatten_kernel(start, v_ref, out_ref, held, came):
    count = held.shape[0]
    loads = [
        pltpu.make_async_copy(
            v_ref.at[pl.ds(start + g, 32)], held.at[pl.ds(g, 32)], came.at[g // 32]
        )
        for g in range(0, count, 32)
    ]
    for load in loads:
        load.start()
    swap = swap_matrix()
    for n, load in enumerate(loads):
        load.wait()
        for p in range(0, 128, 16):
            pair = [
                held[n * 32 + g : n * 32 + g + 16, p : p + 16, :].reshape(256, 128)
                for g in (0, 16)
            ]
            both = jnp.dot(
                swap, jnp.concatenate(pair, axis=1), preferred_element_type=F32
            ).astype(BF)
            for q in range(16):
                for h in range(2):
                    row = n * 32 + h * 16
                    out_ref[row : row + 16, (p + q) * 128 : (p + q + 1) * 128] = both[
                        q * 16 : q * 16 + 16, h * 128 : h * 128 + 128
                    ]


def flatten_vectors(vectors, start, count):
    return pl.pallas_call(
        functools.partial(flatten_kernel, start),
        in_specs=[pl.BlockSpec(memory_space=pl.ANY)],
        out_specs=WHOLE,
        out_shape=pltpu.VMEM((count, 16384), BF),
        scratch_shapes=[
            pltpu.VMEM((count, 128, 128), BF),
            pltpu.SemaphoreType.DMA((count // 32,)),
        ],
        compiler_params=pltpu.CompilerParams(vmem_limit_bytes=10 << 20),
        cost_estimate=pl.CostEstimate(
            flops=2 * count * 16384 * 256, bytes_accessed=4 * count * 16384, transcendentals=0
        ),
    )(pltpu.with_memory_space_constraint(vectors, pltpu.HBM))


def pack_kernel(walk_ref, inv_ref, out_ref):
    out_ref[:, 0:128, :] = walk_ref[...]
    for w in range(16):
        blocks = [inv_ref[w, 32 * n : 32 * n + 32, :] for n in range(4)]
        out_ref[w, 128:160, :] = jnp.concatenate(blocks, axis=1)


def pack(walkers, inverse):
    return pl.pallas_call(
        pack_kernel,
        in_specs=[WHOLE] * 2,
        out_specs=WHOLE,
        out_shape=pltpu.VMEM((16, 160, 128), BF),
        compiler_params=pltpu.CompilerParams(vmem_limit_bytes=6 << 20),
        cost_estimate=pl.CostEstimate(flops=0, bytes_accessed=2 << 20, transcendentals=0),
    )(walkers, inverse.reshape(16, 128, 32))


def theta_kernel(*refs):
    refs, out_ref, work = refs[:-2], refs[-2], refs[-1]
    swap = swap_matrix()
    lane = lax.broadcasted_iota(jnp.int32, (32, 128), 1)
    sign = jnp.where(lane < 64, 1.0, -1.0)
    keep0 = jnp.where(lane % 64 < 32, 1.0, 0.0)
    keep1 = 1.0 - keep0
    size = 16 // len(refs)
    for w in range(16):
        ref = refs[w // size]
        small = ref[w % size, 128:160, :].astype(F32)
        a = small * sign
        b = -jnp.concatenate([small[:, 64:], small[:, :64]], axis=1)
        operator = jnp.concatenate([a * keep0, a * keep1, b * keep0, b * keep1], axis=0).astype(BF)
        work[w] = jnp.dot(
            ref[w % size, 0:128, :], operator, preferred_element_type=F32
        ).astype(BF)
    for p in range(0, 128, 32):
        pair = [work[:, q : q + 16, :].reshape(256, 128) for q in (p, p + 16)]
        both = jnp.dot(
            swap, jnp.concatenate(pair, axis=1), preferred_element_type=F32
        ).astype(BF)
        for h in range(2):
            for q in range(16):
                at = (p + h * 16 + q) * 128
                out_ref[:, at : at + 128] = both[q * 16 : q * 16 + 16, h * 128 : h * 128 + 128]


def theta_of(*pieces):
    return pl.pallas_call(
        theta_kernel,
        in_specs=[WHOLE] * len(pieces),
        out_specs=WHOLE,
        out_shape=pltpu.VMEM((16, 16384), BF),
        scratch_shapes=[pltpu.VMEM((16, 128, 128), BF)],
        compiler_params=pltpu.CompilerParams(vmem_limit_bytes=6 << 20),
        cost_estimate=pl.CostEstimate(
            flops=2 * 16 * 16384 * 256, bytes_accessed=2 << 20, transcendentals=0
        ),
    )(*[near(piece) for piece in pieces])


OFFSETS = ((0, 0), (1, 0), (0, -1), (0, 1), (0, 2), (1, -1), (1, 1), (1, 2))


def place():
    me = lax.axis_index("walk")
    return me >> 3, me >> 1 & 3, me & 1


def product_kernel(part, *refs):
    flats, thetas, source_ref = refs[:4], refs[4:12], refs[12]
    rest = refs[13:]
    acc = rest[-1]
    depth = 4096
    for start in range(0, 16384, depth):
        span = slice(start, start + depth)
        first = jnp.concatenate([t[:, span] for t in thetas], axis=0)
        turned = []
        for n in range(0, depth, 128):
            turned += [-first[:, n + 64 : n + 128], first[:, n : n + 64]]
        both = jnp.concatenate([first, jnp.concatenate(turned, axis=1)], axis=0)
        flat = jnp.concatenate([f[:, span] for f in flats], axis=0)
        product = lax.dot_general(
            flat, both, (((1,), (1,)), ((), ())), preferred_element_type=F32
        )
        if start == 0:
            acc[...] = product
        else:
            acc[...] += product
    bias = acc[...].astype(BF)

    vec = lax.axis_index("vec")
    row = lax.broadcasted_iota(jnp.int32, (256, 256), 0)
    col = lax.broadcasted_iota(jnp.int32, (256, 256), 1)
    target = (((vec >> 1) + (row >> 6)) & 3) * 2 + ((vec + (row >> 5)) & 1)
    sources = jnp.concatenate([source_ref[0:1, :], source_ref[1:2, :]], axis=1)
    found = jnp.where(col == target * 32 + (row & 31), jnp.broadcast_to(sources, (256, 256)), 0)
    wanted = jnp.sum(found, axis=1, keepdims=True)
    x, z, core = place()
    slot = lax.broadcasted_iota(jnp.int32, (256, 128), 1)
    dx, dz = jnp.zeros_like(slot), jnp.zeros_like(slot)
    for n, (sx, sz) in enumerate(OFFSETS[part * 4 : part * 4 + 4]):
        here = (slot >> 4 & 3) == n
        dx = jnp.where(here, sx, dx)
        dz = jnp.where(here, sz, dz)
    old = ((x ^ dx) * 4 + (z + dz & 3)) * 32 + ((core ^ (slot >> 6)) * 16 + (slot & 15))
    pick = jnp.where(wanted == old, 1.0, 0.0).astype(BF)
    for c in range(2):
        picked = lax.dot_general(
            pick,
            bias[:, c * 128 : c * 128 + 128],
            (((1,), (1,)), ((), ())),
            preferred_element_type=F32,
        )
        if part == 0:
            rest[0][c] = picked
        else:
            picked = picked + rest[0][c]
            rest[1][c] = picked[0:32]
            for n in range(1, 8):
                rest[n + 1][c] = picked[n * 32 : n * 32 + 32].astype(BF)


def product(part, flats, thetas, sources, before):
    count = sum(f.shape[0] for f in flats)
    if part:
        shapes = [pltpu.VMEM((2, 32, count), F32)] + [pltpu.VMEM((2, 32, count), BF)] * 7
    else:
        shapes = [pltpu.VMEM((2, 256, count), F32)]
    operands = [near(a) for a in [*flats, *thetas, sources, *before]]
    return pl.pallas_call(
        functools.partial(product_kernel, part),
        in_specs=[WHOLE] * len(operands),
        out_specs=[WHOLE] * len(shapes),
        out_shape=shapes,
        scratch_shapes=[pltpu.VMEM((count, 256), F32)],
        compiler_params=pltpu.CompilerParams(vmem_limit_bytes=14 << 20),
        cost_estimate=pl.CostEstimate(
            flops=2 * count * 16384 * 256, bytes_accessed=2 * (count + 256) * 16384, transcendentals=0
        ),
    )(*operands)


def choose_kernel(source_ref, *refs):
    pieces, outs, table, came, went = refs[:-5], refs[-5:-3], refs[-3], refs[-2], refs[-1]
    loads, base = [], 0
    for n, src in enumerate(pieces):
        size = src.shape[0]
        loads.append(
            pltpu.make_async_copy(
                src.at[:, pl.ds(0, 128), :], table.at[pl.ds(base, size)], came.at[n]
            )
        )
        base += size
    for load in loads:
        load.start()
    x, z, core = place()
    me = lax.axis_index("walk")
    slots = []
    for j in range(32):
        source = source_ref[(me ^ (j // 16)) * 16 + j % 16]
        dx, dz = x ^ (source >> 7), ((source >> 5) - z) & 3
        piece = jnp.int32(0)
        for n, (sx, sz) in enumerate(OFFSETS):
            piece = jnp.where((dx == sx) & (dz == sz % 4), n, piece)
        slots.append(piece * 16 + (source & 15))
    for load in loads:
        load.wait()
    stores = [
        pltpu.make_async_copy(table.at[slots[j]], outs[j // 16].at[j % 16], went.at[j])
        for j in range(32)
    ]
    for store in stores:
        store.start()
    for store in stores:
        store.wait()


def choose(sources, pieces):
    shape = pltpu.VMEM((16, 128, 128), BF)
    return pl.pallas_call(
        choose_kernel,
        in_specs=[pl.BlockSpec(memory_space=pltpu.SMEM)] + [WHOLE] * len(pieces),
        out_specs=[WHOLE] * 2,
        scratch_shapes=[
            pltpu.VMEM((128, 128, 128), BF),
            pltpu.SemaphoreType.DMA((len(pieces),)),
            pltpu.SemaphoreType.DMA((32,)),
        ],
        out_shape=[shape, shape],
        compiler_params=pltpu.CompilerParams(vmem_limit_bytes=8 << 20),
        cost_estimate=pl.CostEstimate(flops=0, bytes_accessed=6 << 20, transcendentals=0),
    )(sources, *[near(piece) for piece in pieces])


def finish_kernel(source_ref, mine_ref, theirs_ref, *refs):
    sums, moved_ref, total_ref = refs[:-2], refs[-2], refs[-1]
    me = lax.axis_index("walk")
    for j in range(16):
        here = (source_ref[me * 16 + j] >> 4 & 1) == (me & 1)
        moved_ref[j] = jnp.where(here, mine_ref[j], theirs_ref[j])
    total = sums[0][...]
    for part in sums[1:]:
        total = total + part[...].astype(F32)
    total_ref[...] = total


def finish(sources, mine, theirs, sums):
    operands = [near(a) for a in [mine, theirs, *sums]]
    return pl.pallas_call(
        finish_kernel,
        in_specs=[pl.BlockSpec(memory_space=pltpu.SMEM)] + [WHOLE] * len(operands),
        out_specs=[WHOLE] * 2,
        out_shape=[
            jax.ShapeDtypeStruct(mine.shape, BF),
            jax.ShapeDtypeStruct(sums[0].shape, F32),
        ],
        compiler_params=pltpu.CompilerParams(vmem_limit_bytes=8 << 20),
        cost_estimate=pl.CostEstimate(flops=0, bytes_accessed=3 << 20, transcendentals=0),
    )(sources, *operands)


def index(x, z, core):
    return (x % 2 * 4 + z % 4) * 2 + core


def moves(step):
    return [
        (index(x, z, c), index(*step(x, z, c))) for x in range(2) for z in range(4) for c in range(2)
    ]


ACROSS = moves(lambda x, z, c: (x + 1, z, c))
UP = moves(lambda x, z, c: (x, z + 1, c))
DOWN = moves(lambda x, z, c: (x, z - 1, c))
OTHER = moves(lambda x, z, c: (x, z, 1 - c))


def send(value, pairs):
    return lax.ppermute(value, "walk", pairs)


def after(values, work):
    return lax.optimization_barrier((values, work))


def per_device(walkers, inverse, vectors, sources):
    own = pack(walkers, inverse)
    first = [send(own, pairs) for pairs in (UP, DOWN, ACROSS)]
    flats = [flatten_vectors(vectors, n * 160, 160) for n in range(4)]
    thetas = [theta_of(own)]
    first, (flats[:3], thetas) = after(first, (flats[:3], thetas))
    below, above, across = first
    far = [send(below[:8], UP), send(above[8:], DOWN)]
    across_below = send(across, UP)
    across_above = send(across, DOWN)
    thetas += [theta_of(piece) for piece in (across, below, above)]
    far, (flats[3], thetas) = after(far, (flats[3], thetas))
    across_far = [send(part, ACROSS) for part in far]
    thetas.append(theta_of(*far))
    thetas = [(t, send(t, OTHER)) for t in thetas]
    short = sources.reshape(2, 128)
    operands = [t[0] for t in thetas[:4]] + [t[1] for t in thetas[:4]]
    sums = product(0, flats, operands, short, [])
    second = [across_below, across_above, across_far]
    second, sums = after(second, sums)
    across_below, across_above, across_far = second
    more = [theta_of(across_below), theta_of(across_above), theta_of(*across_far)]
    thetas += [(t, send(t, OTHER)) for t in more]
    operands = [t[0] for t in thetas[4:]] + [t[1] for t in thetas[4:]]
    pieces = [own, across, below, above, *far, across_below, across_above, *across_far]
    mine, theirs = choose(sources, pieces)
    sums = list(product(1, flats, operands, short, sums))

    for k in range(1, 8):
        pairs = [
            (y * 2 + v, ((y + k // 2) % 4) * 2 + (v + k) % 2) for y in range(4) for v in range(2)
        ]
        sums[k] = lax.ppermute(sums[k], "vec", pairs)
    return tuple(finish(sources, mine, send(theirs, OTHER), sums))


def solution(mesh):
    in_specs = (
        P("walk", "vec", None),
        P("walk", None, None, None, None),
        P("walk", "vec", None),
        P(),
    )
    out_specs = (P("walk", "vec", None), P(None, "vec", "walk"))
    return jax.shard_map(
        per_device, mesh=mesh, in_specs=in_specs, out_specs=out_specs, check_vma=False
    )
```

```python
import functools

import jax
import jax.numpy as jnp
from jax import lax
from jax.experimental import pallas as pl
from jax.experimental.pallas import tpu as pltpu
from jax.sharding import PartitionSpec as P

BF = jnp.bfloat16
F32 = jnp.float32
WHOLE = pl.BlockSpec(memory_space=pltpu.VMEM)
SHORT = pl.CostEstimate(flops=0, bytes_accessed=1024, transcendentals=0)


def near(value):
    return pltpu.with_memory_space_constraint(value, pltpu.VMEM)


def swap_matrix():
    row = lax.broadcasted_iota(jnp.int32, (256, 256), 0)
    col = lax.broadcasted_iota(jnp.int32, (256, 256), 1)
    hit = (row // 16 == col % 16) & (row % 16 == col // 16)
    return jnp.where(hit, 1.0, 0.0).astype(BF)


def flatten_kernel(start, v_ref, out_ref, held, came):
    count = held.shape[0]
    loads = [
        pltpu.make_async_copy(
            v_ref.at[pl.ds(start + g, 32)], held.at[pl.ds(g, 32)], came.at[g // 32]
        )
        for g in range(0, count, 32)
    ]
    for load in loads:
        load.start()
    swap = swap_matrix()
    for n, load in enumerate(loads):
        load.wait()
        for p in range(0, 128, 16):
            pair = [
                held[n * 32 + g : n * 32 + g + 16, p : p + 16, :].reshape(256, 128)
                for g in (0, 16)
            ]
            both = jnp.dot(
                swap, jnp.concatenate(pair, axis=1), preferred_element_type=F32
            ).astype(BF)
            for q in range(16):
                for h in range(2):
                    row = n * 32 + h * 16
                    out_ref[row : row + 16, (p + q) * 128 : (p + q + 1) * 128] = both[
                        q * 16 : q * 16 + 16, h * 128 : h * 128 + 128
                    ]


def flatten_vectors(vectors, start, count):
    return pl.pallas_call(
        functools.partial(flatten_kernel, start),
        in_specs=[pl.BlockSpec(memory_space=pl.ANY)],
        out_specs=WHOLE,
        out_shape=pltpu.VMEM((count, 16384), BF),
        scratch_shapes=[
            pltpu.VMEM((count, 128, 128), BF),
            pltpu.SemaphoreType.DMA((count // 32,)),
        ],
        compiler_params=pltpu.CompilerParams(vmem_limit_bytes=10 << 20),
        cost_estimate=SHORT,
    )(pltpu.with_memory_space_constraint(vectors, pltpu.HBM))


def pack_kernel(walk_ref, inv_ref, out_ref, held, came):
    walk = pltpu.make_async_copy(walk_ref, out_ref.at[:, pl.ds(0, 128), :], came.at[0])
    inverse = pltpu.make_async_copy(inv_ref, held, came.at[1])
    inverse.start()
    walk.start()
    inverse.wait()
    for w in range(16):
        blocks = [held[w, 32 * n : 32 * n + 32, :] for n in range(4)]
        out_ref[w, 128:160, :] = jnp.concatenate(blocks, axis=1)
    walk.wait()


def pack(walkers, inverse):
    inputs = [walkers, inverse.reshape(16, 128, 32)]
    return pl.pallas_call(
        pack_kernel,
        in_specs=[pl.BlockSpec(memory_space=pl.ANY)] * 2,
        out_specs=WHOLE,
        out_shape=pltpu.VMEM((16, 160, 128), BF),
        scratch_shapes=[pltpu.VMEM((16, 128, 32), BF), pltpu.SemaphoreType.DMA((2,))],
        compiler_params=pltpu.CompilerParams(vmem_limit_bytes=6 << 20),
        cost_estimate=SHORT,
    )(*[pltpu.with_memory_space_constraint(a, pltpu.HBM) for a in inputs])


def theta_kernel(*refs):
    refs, out_ref, work = refs[:-2], refs[-2], refs[-1]
    swap = swap_matrix()
    lane = lax.broadcasted_iota(jnp.int32, (32, 128), 1)
    sign = jnp.where(lane < 64, 1.0, -1.0)
    keep0 = jnp.where(lane % 64 < 32, 1.0, 0.0)
    keep1 = 1.0 - keep0
    size = 16 // len(refs)
    for w in range(16):
        ref = refs[w // size]
        small = ref[w % size, 128:160, :].astype(F32)
        a = small * sign
        b = -jnp.concatenate([small[:, 64:], small[:, :64]], axis=1)
        operator = jnp.concatenate([a * keep0, a * keep1, b * keep0, b * keep1], axis=0).astype(BF)
        work[w] = jnp.dot(
            ref[w % size, 0:128, :], operator, preferred_element_type=F32
        ).astype(BF)
    for p in range(0, 128, 32):
        pair = [work[:, q : q + 16, :].reshape(256, 128) for q in (p, p + 16)]
        both = jnp.dot(
            swap, jnp.concatenate(pair, axis=1), preferred_element_type=F32
        ).astype(BF)
        for h in range(2):
            for q in range(16):
                at = (p + h * 16 + q) * 128
                out_ref[:, at : at + 128] = both[q * 16 : q * 16 + 16, h * 128 : h * 128 + 128]


def theta_of(*pieces):
    return pl.pallas_call(
        theta_kernel,
        in_specs=[WHOLE] * len(pieces),
        out_specs=WHOLE,
        out_shape=pltpu.VMEM((16, 16384), BF),
        scratch_shapes=[pltpu.VMEM((16, 128, 128), BF)],
        compiler_params=pltpu.CompilerParams(vmem_limit_bytes=6 << 20),
        cost_estimate=SHORT,
    )(*[near(piece) for piece in pieces])


OFFSETS = ((0, 0), (1, 0), (0, -1), (0, 1), (0, 2), (1, -1), (1, 1), (1, 2))


def place():
    me = lax.axis_index("walk")
    return me >> 3, me >> 1 & 3, me & 1


def product_kernel(part, *refs):
    flats, thetas, source_ref = refs[:4], refs[4:12], refs[12]
    rest = refs[13:]
    acc = rest[-1]
    depth = 4096
    for start in range(0, 16384, depth):
        span = slice(start, start + depth)
        first = jnp.concatenate([t[:, span] for t in thetas], axis=0)
        turned = []
        for n in range(0, depth, 128):
            turned += [-first[:, n + 64 : n + 128], first[:, n : n + 64]]
        both = jnp.concatenate([first, jnp.concatenate(turned, axis=1)], axis=0)
        flat = jnp.concatenate([f[:, span] for f in flats], axis=0)
        product = lax.dot_general(
            flat, both, (((1,), (1,)), ((), ())), preferred_element_type=F32
        )
        if start == 0:
            acc[...] = product
        else:
            acc[...] += product
    bias = acc[...].astype(BF)

    vec = lax.axis_index("vec")
    row = lax.broadcasted_iota(jnp.int32, (256, 256), 0)
    col = lax.broadcasted_iota(jnp.int32, (256, 256), 1)
    target = (((vec >> 1) + (row >> 6)) & 3) * 2 + ((vec + (row >> 5)) & 1)
    sources = jnp.concatenate([source_ref[0:1, :], source_ref[1:2, :]], axis=1)
    found = jnp.where(col == target * 32 + (row & 31), jnp.broadcast_to(sources, (256, 256)), 0)
    wanted = jnp.sum(found, axis=1, keepdims=True)
    x, z, core = place()
    slot = lax.broadcasted_iota(jnp.int32, (256, 128), 1)
    dx, dz = jnp.zeros_like(slot), jnp.zeros_like(slot)
    for n, (sx, sz) in enumerate(OFFSETS[part * 4 : part * 4 + 4]):
        here = (slot >> 4 & 3) == n
        dx = jnp.where(here, sx, dx)
        dz = jnp.where(here, sz, dz)
    old = ((x ^ dx) * 4 + (z + dz & 3)) * 32 + ((core ^ (slot >> 6)) * 16 + (slot & 15))
    pick = jnp.where(wanted == old, 1.0, 0.0).astype(BF)
    for c in range(2):
        picked = lax.dot_general(
            pick,
            bias[:, c * 128 : c * 128 + 128],
            (((1,), (1,)), ((), ())),
            preferred_element_type=F32,
        )
        if part == 0:
            rest[0][c] = picked
        else:
            picked = picked + rest[0][c]
            rest[1][c] = picked[0:32]
            for n in range(1, 8):
                rest[n + 1][c] = picked[n * 32 : n * 32 + 32].astype(BF)


def product(part, flats, thetas, sources, before):
    count = sum(f.shape[0] for f in flats)
    if part:
        shapes = [pltpu.VMEM((2, 32, count), F32)] + [pltpu.VMEM((2, 32, count), BF)] * 7
    else:
        shapes = [pltpu.VMEM((2, 256, count), F32)]
    operands = [near(a) for a in [*flats, *thetas, sources, *before]]
    return pl.pallas_call(
        functools.partial(product_kernel, part),
        in_specs=[WHOLE] * len(operands),
        out_specs=[WHOLE] * len(shapes),
        out_shape=shapes,
        scratch_shapes=[pltpu.VMEM((count, 256), F32)],
        compiler_params=pltpu.CompilerParams(vmem_limit_bytes=14 << 20),
        cost_estimate=SHORT,
    )(*operands)


def choose_kernel(source_ref, *refs):
    pieces, outs, table, came, went = refs[:-5], refs[-5:-3], refs[-3], refs[-2], refs[-1]
    loads, base = [], 0
    for n, src in enumerate(pieces):
        size = src.shape[0]
        loads.append(
            pltpu.make_async_copy(
                src.at[:, pl.ds(0, 128), :], table.at[pl.ds(base, size)], came.at[n]
            )
        )
        base += size
    for load in loads:
        load.start()
    x, z, core = place()
    me = lax.axis_index("walk")
    slots = []
    for j in range(32):
        source = source_ref[(me ^ (j // 16)) * 16 + j % 16]
        dx, dz = x ^ (source >> 7), ((source >> 5) - z) & 3
        piece = jnp.int32(0)
        for n, (sx, sz) in enumerate(OFFSETS):
            piece = jnp.where((dx == sx) & (dz == sz % 4), n, piece)
        slots.append(piece * 16 + (source & 15))
    for load in loads:
        load.wait()
    stores = [
        pltpu.make_async_copy(table.at[slots[j]], outs[j // 16].at[j % 16], went.at[j])
        for j in range(32)
    ]
    for store in stores:
        store.start()
    for store in stores:
        store.wait()


def choose(sources, pieces):
    shape = pltpu.VMEM((16, 128, 128), BF)
    return pl.pallas_call(
        choose_kernel,
        in_specs=[pl.BlockSpec(memory_space=pltpu.SMEM)] + [WHOLE] * len(pieces),
        out_specs=[WHOLE] * 2,
        scratch_shapes=[
            pltpu.VMEM((128, 128, 128), BF),
            pltpu.SemaphoreType.DMA((len(pieces),)),
            pltpu.SemaphoreType.DMA((32,)),
        ],
        out_shape=[shape, shape],
        compiler_params=pltpu.CompilerParams(vmem_limit_bytes=8 << 20),
        cost_estimate=SHORT,
    )(sources, *[near(piece) for piece in pieces])


def finish_kernel(source_ref, mine_ref, theirs_ref, *refs):
    sums, moved_ref, total_ref = refs[:-2], refs[-2], refs[-1]
    me = lax.axis_index("walk")
    for j in range(16):
        here = (source_ref[me * 16 + j] >> 4 & 1) == (me & 1)
        moved_ref[j] = jnp.where(here, mine_ref[j], theirs_ref[j])
    total = sums[0][...]
    for part in sums[1:]:
        total = total + part[...].astype(F32)
    total_ref[...] = total


def finish(sources, mine, theirs, sums):
    operands = [near(a) for a in [mine, theirs, *sums]]
    return pl.pallas_call(
        finish_kernel,
        in_specs=[pl.BlockSpec(memory_space=pltpu.SMEM)] + [WHOLE] * len(operands),
        out_specs=[WHOLE] * 2,
        out_shape=[
            jax.ShapeDtypeStruct(mine.shape, BF),
            jax.ShapeDtypeStruct(sums[0].shape, F32),
        ],
        compiler_params=pltpu.CompilerParams(vmem_limit_bytes=8 << 20),
        cost_estimate=SHORT,
    )(sources, *operands)


def index(x, z, core):
    return (x % 2 * 4 + z % 4) * 2 + core


def moves(step):
    return [
        (index(x, z, c), index(*step(x, z, c))) for x in range(2) for z in range(4) for c in range(2)
    ]


ACROSS = moves(lambda x, z, c: (x + 1, z, c))
UP = moves(lambda x, z, c: (x, z + 1, c))
DOWN = moves(lambda x, z, c: (x, z - 1, c))
OTHER = moves(lambda x, z, c: (x, z, 1 - c))


def send(value, pairs):
    return lax.ppermute(value, "walk", pairs)


def after(values, work):
    return lax.optimization_barrier((values, work))


def per_device(walkers, inverse, vectors, sources):
    own = pack(walkers, inverse)
    first = [send(own, pairs) for pairs in (UP, DOWN, ACROSS)]
    flats = [flatten_vectors(vectors, n * 160, 160) for n in range(4)]
    thetas = [theta_of(own)]
    first, (flats[:3], thetas) = after(first, (flats[:3], thetas))
    below, above, across = first
    far = [send(below[:8], UP), send(above[8:], DOWN)]
    across_below = send(across, UP)
    across_above = send(across, DOWN)
    thetas += [theta_of(piece) for piece in (across, below, above)]
    far, (flats[3], thetas) = after(far, (flats[3], thetas))
    across_far = [send(part, ACROSS) for part in far]
    thetas.append(theta_of(*far))
    thetas = [(t, send(t, OTHER)) for t in thetas]
    short = sources.reshape(2, 128)
    operands = [t[0] for t in thetas[:4]] + [t[1] for t in thetas[:4]]
    sums = product(0, flats, operands, short, [])
    second = [across_below, across_above]
    second, sums = after(second, sums)
    across_below, across_above = second
    more = [theta_of(piece) for piece in second]
    across_far, more = after(across_far, more)
    more.append(theta_of(*across_far))
    thetas += [(t, send(t, OTHER)) for t in more]
    operands = [t[0] for t in thetas[4:]] + [t[1] for t in thetas[4:]]
    pieces = [own, across, below, above, *far, across_below, across_above, *across_far]
    mine, theirs = choose(sources, pieces)
    sums = list(product(1, flats, operands, short, sums))

    for k in range(1, 8):
        pairs = [
            (y * 2 + v, ((y + k // 2) % 4) * 2 + (v + k) % 2) for y in range(4) for v in range(2)
        ]
        sums[k] = lax.ppermute(sums[k], "vec", pairs)
    return tuple(finish(sources, mine, send(theirs, OTHER), sums))


def solution(mesh):
    in_specs = (
        P("walk", "vec", None),
        P("walk", None, None, None, None),
        P("walk", "vec", None),
        P(),
    )
    out_specs = (P("walk", "vec", None), P(None, "vec", "walk"))
    return jax.shard_map(
        per_device, mesh=mesh, in_specs=in_specs, out_specs=out_specs, check_vma=False
    )
```
